512 devices in a mesh: seq: 16 (over y, core), wide: 32 (over z, x).
Axes of the slice: x: 4, y: 8, z: 8, core: 2. Of those that a mesh axis runs over, the one named last changes fastest.
Arguments:
- out_gate: bfloat16 [65536, 4096], P(('seq', 'wide')), may hold values from -6 to 6
- in_gate: bfloat16 [65536, 4096], P(('seq', 'wide')), may hold values from -6 to 6
- values: bfloat16 [65536, 4096], P(('seq', 'wide')), may hold values from -6 to 6
- filter_taps: bfloat16 [4096, 4096], P('seq', 'wide'), may hold values from -0.09375 to 0.09375
- skip_gain: float32 [4096], P('wide'), may hold values from 0.5 to 1.5
Outputs:
- mixed: bfloat16 [65536, 4096], P(('seq', 'wide'))
The draws below stay inside these ranges and needn't reach their ends.
All inputs are finite; a program needn't handle non-finite values.
Results may differ from the reference program's by a relative error of at most 0.0065.
Values may be sent and summed in bfloat16 or wider, within the bound.
A program may use at most 64 MiB of HBM per device.

```python
import jax
import jax.numpy as jnp
from jax import lax

D = 4096
TAPS = 4096
LENGTH = 65536


def block_levels(key, shape, cuts, smallest, top_value):
    level, own = 1.0, jax.random.fold_in(key, 6)
    for position, blocks in cuts:
        draws = jnp.exp(jax.random.uniform(jax.random.fold_in(own, position), (blocks,), jnp.float32, smallest / len(cuts), top_value / len(cuts)))
        level = level * jnp.repeat(draws, shape[position] // blocks).reshape([-1 if axis == position else 1 for axis in range(len(shape))])
    return level


def centred(key, extent, width, limit, split=(), held_as=jnp.bfloat16):
    loudness = block_levels(key, extent, split, -0.22, 0.18) if split else 1.0
    array = jax.random.normal(key, extent, jnp.float32) * width * loudness
    return jnp.minimum(jnp.maximum(array, -limit), limit).astype(held_as)


def setup_inputs(seed: int = 0) -> dict:
    key_of = jax.random.split(jax.random.key(seed), 6)
    return {
        "out_gate": centred(key_of[0], (LENGTH, D), 1.0, 6.0, ((0, 512),)),
        "in_gate": centred(key_of[1], (LENGTH, D), 1.0, 6.0, ((0, 512),)),
        "values": centred(key_of[2], (LENGTH, D), 1.0, 6.0, ((0, 512),)),
        "filter_taps": centred(key_of[3], (TAPS, D), TAPS ** -0.5, 0.09375, ((0, 16), (1, 32))),
        "skip_gain": jnp.clip(0.5 + 1.0 * jax.random.uniform(key_of[4], (D,), jnp.float32) ** block_levels(key_of[4], (D,), ((0, 32),), -0.2, 0.2), 0.5, 1.5),
    }


def reference(out_gate, in_gate, values, filter_taps, skip_gain):
    length = out_gate.shape[0]
    model_width = out_gate.shape[1]
    tap_count = filter_taps.shape[0]
    block_width = min(256, model_width)
    block_count = model_width // block_width
    padded_length = length + tap_count

    def one_block(block_index):
        offset = block_index * block_width
        gate_block = lax.dynamic_slice_in_dim(in_gate, offset, block_width, 1).astype(jnp.float32)
        value_block = lax.dynamic_slice_in_dim(values, offset, block_width, 1).astype(jnp.float32)
        output_block = lax.dynamic_slice_in_dim(out_gate, offset, block_width, 1).astype(jnp.float32)
        tap_block = lax.dynamic_slice_in_dim(filter_taps, offset, block_width, 1).astype(jnp.float32)
        skip_block = lax.dynamic_slice_in_dim(skip_gain, offset, block_width, 0)
        gated_values = (gate_block * value_block).astype(jnp.bfloat16)
        gated_values = lax.optimization_barrier(gated_values).astype(jnp.float32)
        spectrum = jnp.fft.rfft(gated_values, n=padded_length, axis=0) * jnp.fft.rfft(tap_block, n=padded_length, axis=0)
        convolved = jnp.fft.irfft(spectrum, n=padded_length, axis=0)[:length]
        filtered = (convolved + skip_block[None, :] * gated_values).astype(jnp.bfloat16)
        filtered = lax.optimization_barrier(filtered).astype(jnp.float32)
        return (output_block * filtered).astype(jnp.bfloat16)

    pieces = lax.map(one_block, jnp.arange(block_count, dtype=jnp.int32))
    return jnp.transpose(pieces, (1, 0, 2)).reshape(length, model_width)
```

```python
import jax
import jax.numpy as jnp
import ml_dtypes
import numpy as np
from jax import lax
from jax.experimental import pallas as pl
from jax.experimental.pallas import tpu as pltpu
from jax.sharding import PartitionSpec as P

MESH = pl.DeviceIdType.MESH
F32, BF16 = jnp.float32, jnp.bfloat16

LANE = 128
BLOCKS = 32
GROUPS = 16
FREQ = 128
WIDE = 64
PITCH = FREQ + 8


def tables():
    k, b, m = np.arange(FREQ), np.arange(LANE), np.arange(WIDE)
    angle = np.pi * (2 * k + 1) / 256
    wide_angle = 2 * np.pi * (np.outer(m, m) % WIDE) / WIDE

    spread = np.outer(angle, b)
    block_in = np.concatenate([np.cos(spread), -np.sin(spread)], 0)
    cosine, sine = np.cos(wide_angle), np.sin(wide_angle)
    wide_in = np.zeros((2, WIDE, WIDE, 2))
    wide_in[0, :, :, 0], wide_in[0, :, :, 1] = cosine, sine
    wide_in[1, :, :, 0], wide_in[1, :, :, 1] = -sine, cosine

    turn = np.exp(-1j * wide_angle)[:, :BLOCKS]
    tap_in = np.zeros((2, 2, WIDE, BLOCKS, 2))
    for parity, sign in ((0, 1.0), (1, -1.0)):
        factor = (1 + 1j * sign * np.exp(-2j * np.pi * m / WIDE))[:, None] * turn
        tap_in[parity, 0, :, :, 0], tap_in[parity, 0, :, :, 1] = factor.real, -factor.imag
        tap_in[parity, 1, :, :, 0], tap_in[parity, 1, :, :, 1] = factor.imag, factor.real

    wide_out = np.zeros((BLOCKS, 2, 2, WIDE))
    cosine, sine = cosine[BLOCKS:], sine[BLOCKS:]
    wide_out[:, 0, 0], wide_out[:, 0, 1] = cosine, -sine
    wide_out[:, 1, 0], wide_out[:, 1, 1] = sine, cosine
    block_out = np.concatenate([np.cos(spread.T), -np.sin(spread.T)], 1)
    made = (
        block_in,
        wide_in.reshape(2 * WIDE, 2 * WIDE),
        tap_in.reshape(2, 2 * WIDE, 2 * BLOCKS),
        wide_out.reshape(2 * BLOCKS, 2 * WIDE) / WIDE,
        block_out / FREQ,
    )
    return [table.astype(np.float32).astype(ml_dtypes.bfloat16) for table in made]


def dot(left, right):
    return jnp.dot(left, right, preferred_element_type=F32)


def rows(start, count=LANE, align=8):
    return pl.ds(pl.multiple_of(start, align), count)


def kernel(
    out_gate, in_gate, values, taps, skip, block_in, wide_in, tap_in, wide_out, block_out,
    result,
    gate_a, gate_b, gate_c, gated, own, before, all_taps, filtered, returned,
    signal_rows, tap_rows, tap_spectrum, product, answer_rows,
    load_sem, go_send, go_recv, pass_send, pass_recv, tap_send, tap_recv, twin_send, twin_recv,
    back_send, back_recv,
):
    s, v = lax.axis_index("seq"), lax.axis_index("wide")
    z, x = v // 4, v % 4
    twin = s + 1 - 2 * (s % 2)

    def ahead(k):
        return (z + k // 4) % 8 * 4 + (x + k % 4) % 4

    def behind(k):
        return (z + 8 - k // 4) % 8 * 4 + (x + 4 - k % 4) % 4

    loads = [
        pltpu.make_async_copy(source, target, load_sem.at[i])
        for i, (source, target) in enumerate(((in_gate, gate_a), (values, gate_b), (out_gate, gate_c)))
    ]
    for load in loads:
        load.start()

    barrier = pltpu.get_barrier_semaphore()

    def greet(k, carry):
        pl.semaphore_signal(barrier, inc=1, device_id={"wide": behind(k)}, device_id_type=MESH)
        return carry

    lax.fori_loop(1, BLOCKS, greet, 0)
    for step in range(1, 8):
        pl.semaphore_signal(
            barrier, inc=1, device_id={"seq": (s + GROUPS - 2 * step) % GROUPS}, device_id_type=MESH
        )
    pl.semaphore_signal(barrier, inc=1, device_id={"seq": twin}, device_id_type=MESH)
    pl.semaphore_signal(barrier, inc=1, device_id={"seq": (s + GROUPS - 1) % GROUPS}, device_id_type=MESH)

    def go(k):
        return pltpu.make_async_remote_copy(
            src_ref=gated.at[ahead(k)], dst_ref=own.at[v],
            send_sem=go_send.at[k], recv_sem=go_recv.at[k],
            device_id={"wide": ahead(k)}, device_id_type=MESH,
        )

    def pass_on(k):
        block = behind(k)
        return pltpu.make_async_remote_copy(
            src_ref=own.at[block], dst_ref=before.at[block],
            send_sem=pass_send.at[k], recv_sem=pass_recv.at[k],
            device_id={"seq": (s + 1) % GROUPS}, device_id_type=MESH,
        )

    def tap_go(i):
        return pltpu.make_async_remote_copy(
            src_ref=all_taps.at[s], dst_ref=all_taps.at[s],
            send_sem=tap_send.at[i], recv_sem=tap_recv.at[i],
            device_id={"seq": (s + 2 * i) % GROUPS}, device_id_type=MESH,
        )

    def tap_twin(i):
        group = (s + GROUPS - 2 * i) % GROUPS
        return pltpu.make_async_remote_copy(
            src_ref=all_taps.at[group], dst_ref=all_taps.at[group],
            send_sem=twin_send.at[i], recv_sem=twin_recv.at[i],
            device_id={"seq": twin}, device_id_type=MESH,
        )

    def back(k):
        return pltpu.make_async_remote_copy(
            src_ref=filtered.at[ahead(k)], dst_ref=returned.at[v],
            send_sem=back_send.at[k], recv_sem=back_recv.at[k],
            device_id={"wide": ahead(k)}, device_id_type=MESH,
        )

    all_taps[s] = taps[...]
    loads[0].wait()
    loads[1].wait()

    def gate(u, carry):
        columns = rows(u * LANE, align=LANE)
        gated[u] = (gate_a[:, columns].astype(F32) * gate_b[:, columns].astype(F32)).astype(BF16)
        return carry

    lax.fori_loop(0, BLOCKS, gate, 0, unroll=2)
    pl.semaphore_wait(barrier, BLOCKS - 1 + 9)

    def send_go(k, carry):
        go(k).start()
        return carry

    lax.fori_loop(1, BLOCKS, send_go, 0)
    tap_twin(0).start()
    for i in range(1, 8):
        tap_go(i).start()
    own[v] = gated[v]

    def block_spectrum(source, target, at):
        spectrum = dot(block_in[...], source)
        target[rows(at * 2 * PITCH), :] = spectrum[:FREQ]
        target[rows(at * 2 * PITCH + PITCH), :] = spectrum[FREQ:]

    pass_on(0).start()
    block_spectrum(own[v], signal_rows, BLOCKS + v)

    def arrive(k, carry):
        go(k).wait_recv()
        pass_on(k).start()
        at = behind(k)
        block_spectrum(own[at], signal_rows, BLOCKS + at)
        return carry

    lax.fori_loop(1, BLOCKS, arrive, 0)

    for i in range(1, 8):
        tap_go(i).wait_recv()
        tap_twin(i).start()
    for i in range(8):
        tap_twin(i).wait_recv()

    def tap_block(g, carry):
        for half in range(2):
            block_spectrum(all_taps[g, half * LANE : (half + 1) * LANE], tap_rows, 2 * g + half)
        return carry

    lax.fori_loop(0, GROUPS, tap_block, 0, unroll=2)

    def pair(source, k, count):
        first = source[pl.ds(k, count, stride=PITCH), :]
        second = source[pl.ds(k + FREQ // 2, count, stride=PITCH), :]
        return jnp.concatenate([first, second], axis=1).astype(BF16)

    def tap_wide(i, carry):
        for p in range(8):
            k = 8 * i + p
            tap_spectrum[k] = dot(tap_in[p % 2], pair(tap_rows, k, 2 * BLOCKS))
        return carry

    lax.fori_loop(0, FREQ // 16, tap_wide, 0)

    def arrive_before(k, carry):
        pass_on(k).wait_recv()
        at = behind(k)
        block = before[at]
        block_spectrum(jnp.where(s > 0, block, jnp.zeros_like(block)), signal_rows, at)
        return carry

    lax.fori_loop(0, BLOCKS, arrive_before, 0)

    def multiply(i, carry):
        for p in range(8):
            k = 8 * i + p
            signal = dot(wide_in[...], pair(signal_rows, k, 2 * WIDE))
            tap = tap_spectrum[k]
            real, imag, tap_real, tap_imag = signal[:WIDE], signal[WIDE:], tap[:WIDE], tap[WIDE:]
            product[k] = jnp.concatenate(
                [real * tap_real - imag * tap_imag, real * tap_imag + imag * tap_real], axis=0
            ).astype(BF16)
        return carry

    lax.fori_loop(0, FREQ // 16, multiply, 0)

    def wide_back(i, carry):
        for p in range(8):
            k = 8 * i + p
            answer = dot(wide_out[...], product[k])
            answer_rows[pl.ds(k, 2 * BLOCKS, stride=PITCH), :] = answer[:, :LANE]
            answer_rows[pl.ds(k + FREQ // 2, 2 * BLOCKS, stride=PITCH), :] = answer[:, LANE:]
        return carry

    lax.fori_loop(0, FREQ // 16, wide_back, 0)

    def finish(i, carry):
        for p in range(4):
            at = ahead(4 * i + p)
            spectrum = jnp.concatenate(
                [answer_rows[rows(at * 2 * PITCH), :], answer_rows[rows(at * 2 * PITCH + PITCH), :]], axis=0
            ).astype(BF16)
            direct = skip[...] * own[at].astype(F32)
            filtered[at] = (dot(block_out[...], spectrum) + direct).astype(BF16)
        for p in range(4):
            @pl.when(4 * i + p > 0)
            def _():
                back(4 * i + p).start()
        return carry

    lax.fori_loop(0, BLOCKS // 4, finish, 0)
    loads[2].wait()
    returned[v] = filtered[v]

    def output(at):
        columns = rows(at * LANE, align=LANE)
        result[:, columns] = (gate_c[:, columns].astype(F32) * returned[at].astype(F32)).astype(BF16)

    output(v)

    def arrive_back(k, carry):
        back(k).wait_recv()
        output(behind(k))
        return carry

    lax.fori_loop(1, BLOCKS, arrive_back, 0)

    def drain(k, carry):
        go(k).wait_send()
        back(k).wait_send()
        pass_on(k).wait_send()
        return carry

    lax.fori_loop(1, BLOCKS, drain, 0)
    pass_on(0).wait_send()
    for i in range(8):
        tap_twin(i).wait_send()
    for i in range(1, 8):
        tap_go(i).wait_send()


def local(out_gate, in_gate, values, filter_taps, skip_gain):
    vmem, anywhere = pl.BlockSpec(memory_space=pltpu.VMEM), pl.BlockSpec(memory_space=pl.ANY)
    block = (BLOCKS, LANE, LANE)
    many, eight = pltpu.SemaphoreType.DMA((BLOCKS,)), pltpu.SemaphoreType.DMA((8,))
    return pl.pallas_call(
        kernel,
        out_shape=jax.ShapeDtypeStruct(out_gate.shape, BF16),
        in_specs=[anywhere] * 3 + [vmem] * 7,
        out_specs=vmem,
        scratch_shapes=[pltpu.VMEM(out_gate.shape, BF16)] * 3
        + [pltpu.VMEM(block, BF16)] * 3
        + [pltpu.VMEM((GROUPS, 2 * LANE, LANE), BF16)]
        + [pltpu.VMEM(block, BF16)] * 2
        + [
            pltpu.VMEM((2 * WIDE * PITCH, LANE), F32),
            pltpu.VMEM((2 * BLOCKS * PITCH, LANE), F32),
            pltpu.VMEM((FREQ // 2, 2 * WIDE, 2 * LANE), F32),
            pltpu.VMEM((FREQ // 2, 2 * WIDE, 2 * LANE), BF16),
            pltpu.VMEM((2 * BLOCKS * PITCH, LANE), F32),
            pltpu.SemaphoreType.DMA((3,)),
            many, many, many, many, eight, eight, eight, eight, many, many,
        ],
        compiler_params=pltpu.CompilerParams(
            collective_id=0, has_side_effects=True, vmem_limit_bytes=58 << 20
        ),
    )(out_gate, in_gate, values, filter_taps, skip_gain[None, :], *tables())


def solution(mesh):
    rows_split = P(("seq", "wide"), None)
    return jax.shard_map(
        local,
        mesh=mesh,
        in_specs=(rows_split, rows_split, rows_split, P("seq", "wide"), P("wide")),
        out_specs=rows_split,
        check_vma=False,
    )
```

```python
import jax
import jax.numpy as jnp
import ml_dtypes
import numpy as np
from jax import lax
from jax.experimental import pallas as pl
from jax.experimental.pallas import tpu as pltpu
from jax.sharding import PartitionSpec as P

MESH = pl.DeviceIdType.MESH
F32, BF16 = jnp.float32, jnp.bfloat16

LANE = 128
BLOCKS = 32
GROUPS = 16
FREQ = 128
WIDE = 64
LAG = 5
PITCH = FREQ + 8


def tables():
    k, b, m = np.arange(FREQ), np.arange(LANE), np.arange(WIDE)
    angle = np.pi * (2 * k + 1) / 256
    wide_angle = 2 * np.pi * (np.outer(m, m) % WIDE) / WIDE

    spread = np.outer(angle, b)
    block_in = np.concatenate([np.cos(spread), -np.sin(spread)], 0)
    cosine, sine = np.cos(wide_angle), np.sin(wide_angle)
    wide_in = np.zeros((2, WIDE, WIDE, 2))
    wide_in[0, :, :, 0], wide_in[0, :, :, 1] = cosine, sine
    wide_in[1, :, :, 0], wide_in[1, :, :, 1] = -sine, cosine

    turn = np.exp(-1j * wide_angle)[:, :BLOCKS]
    tap_in = np.zeros((2, 2, WIDE, BLOCKS, 2))
    for parity, sign in ((0, 1.0), (1, -1.0)):
        factor = (1 + 1j * sign * np.exp(-2j * np.pi * m / WIDE))[:, None] * turn
        tap_in[parity, 0, :, :, 0], tap_in[parity, 0, :, :, 1] = factor.real, -factor.imag
        tap_in[parity, 1, :, :, 0], tap_in[parity, 1, :, :, 1] = factor.imag, factor.real

    wide_out = np.zeros((BLOCKS, 2, 2, WIDE))
    cosine, sine = cosine[BLOCKS:], sine[BLOCKS:]
    wide_out[:, 0, 0], wide_out[:, 0, 1] = cosine, -sine
    wide_out[:, 1, 0], wide_out[:, 1, 1] = sine, cosine
    block_out = np.concatenate([np.cos(spread.T), -np.sin(spread.T)], 1)
    made = (
        block_in,
        wide_in.reshape(2 * WIDE, 2 * WIDE),
        tap_in.reshape(2, 2 * WIDE, 2 * BLOCKS),
        wide_out.reshape(2 * BLOCKS, 2 * WIDE) / WIDE,
        block_out / FREQ,
    )
    return [table.astype(np.float32).astype(ml_dtypes.bfloat16) for table in made]


def dot(left, right):
    return jnp.dot(left, right, preferred_element_type=F32)


def rows(start, count=LANE, align=8):
    return pl.ds(pl.multiple_of(start, align), count)


def kernel(
    in_gate, values, taps, skip, *rest
):
    table_refs, rest = rest[:5], rest[5:]
    result, gate_a, gate_b, skip_here, *rest = rest
    (block_in, wide_in, tap_in, wide_out, block_out), rest = rest[:5], rest[5:]
    (
        gated, own, before, all_taps, filtered, returned,
        signal_rows, tap_rows, tap_spectrum, product, answer_rows,
        load_sem, go_send, go_recv, pass_send, pass_recv, tap_send, tap_recv, twin_send, twin_recv,
        back_send, back_recv,
    ) = rest
    s, v = lax.axis_index("seq"), lax.axis_index("wide")
    z, x = v // 4, v % 4
    twin = s + 1 - 2 * (s % 2)

    def near(i):
        return (8 + (2 * (i % 2) - 1) * ((i + 1) // 2)) % 8

    def ahead(k):
        return (z + k // 4) % 8 * 4 + (x + k % 4) % 4

    def behind(k):
        return (z + 8 - k // 4) % 8 * 4 + (x + 4 - k % 4) % 4

    here = (in_gate, values, taps, *table_refs, skip)
    there = (gate_a, gate_b, all_taps.at[s], block_in, wide_in, tap_in, wide_out, block_out, skip_here)
    loads = [
        pltpu.make_async_copy(source, target, load_sem.at[i])
        for i, (source, target) in enumerate(zip(here, there))
    ]
    for load in loads:
        load.start()

    barrier = pltpu.get_barrier_semaphore()

    def greet(k, carry):
        pl.semaphore_signal(barrier, inc=1, device_id={"wide": behind(k)}, device_id_type=MESH)
        return carry

    lax.fori_loop(1, BLOCKS, greet, 0)
    for step in range(1, 8):
        pl.semaphore_signal(
            barrier, inc=1, device_id={"seq": (s + GROUPS - 2 * step) % GROUPS}, device_id_type=MESH
        )
    pl.semaphore_signal(barrier, inc=1, device_id={"seq": twin}, device_id_type=MESH)
    pl.semaphore_signal(barrier, inc=1, device_id={"seq": (s + GROUPS - 1) % GROUPS}, device_id_type=MESH)

    def go(k):
        return pltpu.make_async_remote_copy(
            src_ref=gated.at[ahead(k)], dst_ref=own.at[v],
            send_sem=go_send.at[k], recv_sem=go_recv.at[k],
            device_id={"wide": ahead(k)}, device_id_type=MESH,
        )

    def pass_on(step):
        blocks = pl.ds((z + 8 - step) % 8 * 4, 4)
        return pltpu.make_async_remote_copy(
            src_ref=own.at[blocks], dst_ref=before.at[blocks],
            send_sem=pass_send.at[step], recv_sem=pass_recv.at[step],
            device_id={"seq": (s + 1) % GROUPS}, device_id_type=MESH,
        )

    def tap_go(i):
        return pltpu.make_async_remote_copy(
            src_ref=all_taps.at[s], dst_ref=all_taps.at[s],
            send_sem=tap_send.at[i], recv_sem=tap_recv.at[i],
            device_id={"seq": (s + 2 * i) % GROUPS}, device_id_type=MESH,
        )

    def tap_twin(i):
        group = (s + GROUPS - 2 * i) % GROUPS
        return pltpu.make_async_remote_copy(
            src_ref=all_taps.at[group], dst_ref=all_taps.at[group],
            send_sem=twin_send.at[i], recv_sem=twin_recv.at[i],
            device_id={"seq": twin}, device_id_type=MESH,
        )

    def back(k):
        return pltpu.make_async_remote_copy(
            src_ref=filtered.at[ahead(k)], dst_ref=returned.at[v],
            send_sem=back_send.at[k], recv_sem=back_recv.at[k],
            device_id={"wide": ahead(k)}, device_id_type=MESH,
        )

    pl.semaphore_wait(barrier, BLOCKS - 1 + 9)
    loads[2].wait()
    for i in range(1, 8):
        tap_go(i).start()
    tap_twin(0).start()
    loads[0].wait()
    loads[1].wait()

    def gate(u):
        columns = rows(u * LANE, align=LANE)
        gated[u] = (gate_a[:, columns].astype(F32) * gate_b[:, columns].astype(F32)).astype(BF16)

    def send_go(i, carry):
        step = near(i)
        for j in range(4):
            k = 4 * step + j
            gate(ahead(k))

            @pl.when(k > 0)
            def _():
                go(k).start()

        return carry

    lax.fori_loop(0, 8, send_go, 0)
    own[v] = gated[v]
    for load in loads[3:]:
        load.wait()

    def block_spectrum(source, target, at):
        spectrum = dot(block_in[...], source)
        target[rows(at * 2 * PITCH), :] = spectrum[:FREQ]
        target[rows(at * 2 * PITCH + PITCH), :] = spectrum[FREQ:]

    def pair(source, k, count):
        first = source[pl.ds(k, count, stride=PITCH), :]
        second = source[pl.ds(k + FREQ // 2, count, stride=PITCH), :]
        return jnp.concatenate([first, second], axis=1).astype(BF16)

    for i in range(1, 8):
        tap_go(i).wait_recv()
        tap_twin(i).start()
    for i in range(8):
        tap_twin(i).wait_recv()

    def tap_block(i, carry):
        for j in range(4):
            block = all_taps[2 * i + j // 2, j % 2 * LANE : (j % 2 + 1) * LANE]
            block_spectrum(block, tap_rows, 4 * i + j)
        return carry

    lax.fori_loop(0, 8, tap_block, 0)

    def tap_wide(i, carry):
        for p in range(16):
            k = 16 * i + p
            tap_spectrum[k] = dot(tap_in[p % 2], pair(tap_rows, k, 2 * BLOCKS))
        return carry

    lax.fori_loop(0, 4, tap_wide, 0)

    def arrive(i):
        step = near(i)
        for j in range(4):
            @pl.when(4 * step + j > 0)
            def _():
                go(4 * step + j).wait_recv()
        pass_on(step).start()
        for j in range(4):
            at = (z + 8 - step) % 8 * 4 + j
            block_spectrum(own[at], signal_rows, BLOCKS + at)

    def arrive_before(i):
        step = near(i)
        pass_on(step).wait_recv()
        for j in range(4):
            at = (z + 8 - step) % 8 * 4 + j
            block = before[at]
            block_spectrum(jnp.where(s > 0, block, jnp.zeros_like(block)), signal_rows, at)

    def first(i, carry):
        arrive(i)
        return carry

    def both(i, carry):
        arrive(i)
        arrive_before(i - LAG)
        return carry

    def last(i, carry):
        arrive_before(i)
        return carry

    lax.fori_loop(0, LAG, first, 0)
    lax.fori_loop(LAG, 8, both, 0)
    lax.fori_loop(8 - LAG, 8, last, 0)

    def multiply(i, carry):
        for p in range(32):
            k = 32 * i + p
            signal = dot(wide_in[...], pair(signal_rows, k, 2 * WIDE))
            tap = tap_spectrum[k]
            real, imag, tap_real, tap_imag = signal[:WIDE], signal[WIDE:], tap[:WIDE], tap[WIDE:]
            product[k] = jnp.concatenate(
                [real * tap_real - imag * tap_imag, real * tap_imag + imag * tap_real], axis=0
            ).astype(BF16)
        return carry

    lax.fori_loop(0, 2, multiply, 0)

    def wide_back(i, carry):
        for p in range(16):
            k = 16 * i + p
            answer = dot(wide_out[...], product[k])
            answer_rows[pl.ds(k, 2 * BLOCKS, stride=PITCH), :] = answer[:, :LANE]
            answer_rows[pl.ds(k + FREQ // 2, 2 * BLOCKS, stride=PITCH), :] = answer[:, LANE:]
        return carry

    lax.fori_loop(0, 4, wide_back, 0)

    def finish(i, carry):
        for p in range(4):
            at = ahead(4 * near(i) + p)
            spectrum = jnp.concatenate(
                [answer_rows[rows(at * 2 * PITCH), :], answer_rows[rows(at * 2 * PITCH + PITCH), :]], axis=0
            ).astype(BF16)
            direct = skip_here[...] * own[at].astype(F32)
            filtered[at] = (dot(block_out[...], spectrum) + direct).astype(BF16)
        for p in range(4):
            k = 4 * near(i) + p

            @pl.when(k > 0)
            def _():
                back(k).start()
        return carry

    lax.fori_loop(0, BLOCKS // 4, finish, 0)
    returned[v] = filtered[v]

    def output(at):
        columns = rows(at * LANE, align=LANE)
        result[:, columns] = returned[at]

    def arrive_back(i, carry):
        for j in range(4):
            k = 4 * near(i) + j

            @pl.when(k > 0)
            def _():
                back(k).wait_recv()

        for j in range(4):
            output(behind(4 * near(i) + j))
        return carry

    lax.fori_loop(0, 8, arrive_back, 0)

    def drain(k, carry):
        go(k).wait_send()
        back(k).wait_send()
        return carry

    lax.fori_loop(1, BLOCKS, drain, 0)
    for i in range(8):
        pass_on(i).wait_send()
    for i in range(8):
        tap_twin(i).wait_send()
    for i in range(1, 8):
        tap_go(i).wait_send()


def local(out_gate, in_gate, values, filter_taps, skip_gain):
    vmem, anywhere = pl.BlockSpec(memory_space=pltpu.VMEM), pl.BlockSpec(memory_space=pl.ANY)
    block = (BLOCKS, LANE, LANE)
    many, eight = pltpu.SemaphoreType.DMA((BLOCKS,)), pltpu.SemaphoreType.DMA((8,))
    made = tables()
    filtered = pl.pallas_call(
        kernel,
        out_shape=jax.ShapeDtypeStruct(out_gate.shape, BF16),
        in_specs=[anywhere] * (4 + len(made)),
        out_specs=vmem,
        scratch_shapes=[pltpu.VMEM(out_gate.shape, BF16)] * 2
        + [pltpu.VMEM((1, LANE), F32)]
        + [pltpu.VMEM(table.shape, BF16) for table in made]
        + [pltpu.VMEM(block, BF16)] * 3
        + [pltpu.VMEM((GROUPS, 2 * LANE, LANE), BF16)]
        + [pltpu.VMEM(block, BF16)] * 2
        + [
            pltpu.VMEM((2 * WIDE * PITCH, LANE), F32),
            pltpu.VMEM((2 * BLOCKS * PITCH, LANE), F32),
            pltpu.VMEM((FREQ // 2, 2 * WIDE, 2 * LANE), F32),
            pltpu.VMEM((FREQ // 2, 2 * WIDE, 2 * LANE), BF16),
            pltpu.VMEM((2 * BLOCKS * PITCH, LANE), F32),
            pltpu.SemaphoreType.DMA((4 + len(made),)),
            many, many, eight, eight, eight, eight, eight, eight, many, many,
        ],
        compiler_params=pltpu.CompilerParams(
            collective_id=0, has_side_effects=True, vmem_limit_bytes=58 << 20
        ),
    )(in_gate, values, filter_taps, skip_gain[None, :], *made)
    return (out_gate.astype(F32) * filtered.astype(F32)).astype(BF16)


def solution(mesh):
    rows_split = P(("seq", "wide"), None)
    return jax.shard_map(
        local,
        mesh=mesh,
        in_specs=(rows_split, rows_split, rows_split, P("seq", "wide"), P("wide")),
        out_specs=rows_split,
        check_vma=False,
    )
```

```python
import jax
import jax.numpy as jnp
import ml_dtypes
import numpy as np
from jax import lax
from jax.experimental import pallas as pl
from jax.experimental.pallas import tpu as pltpu
from jax.sharding import PartitionSpec as P

MESH = pl.DeviceIdType.MESH
F32, BF16 = jnp.float32, jnp.bfloat16

LANE = 128
BLOCKS = 32
GROUPS = 16
FREQ = 128
WIDE = 64
LAG = 5
PITCH = FREQ + 8


def tables():
    k, b, m = np.arange(FREQ), np.arange(LANE), np.arange(WIDE)
    angle = np.pi * (2 * k + 1) / 256
    wide_angle = 2 * np.pi * (np.outer(m, m) % WIDE) / WIDE

    spread = np.outer(angle, b)
    block_in = np.concatenate([np.cos(spread), -np.sin(spread)], 0)
    cosine, sine = np.cos(wide_angle), np.sin(wide_angle)
    wide_in = np.zeros((2, WIDE, WIDE, 2))
    wide_in[0, :, :, 0], wide_in[0, :, :, 1] = cosine, sine
    wide_in[1, :, :, 0], wide_in[1, :, :, 1] = -sine, cosine

    turn = np.exp(-1j * wide_angle)[:, :BLOCKS]
    tap_in = np.zeros((2, 2, WIDE, BLOCKS, 2))
    for parity, sign in ((0, 1.0), (1, -1.0)):
        factor = (1 + 1j * sign * np.exp(-2j * np.pi * m / WIDE))[:, None] * turn
        tap_in[parity, 0, :, :, 0], tap_in[parity, 0, :, :, 1] = factor.real, -factor.imag
        tap_in[parity, 1, :, :, 0], tap_in[parity, 1, :, :, 1] = factor.imag, factor.real

    wide_out = np.zeros((BLOCKS, 2, 2, WIDE))
    cosine, sine = cosine[BLOCKS:], sine[BLOCKS:]
    wide_out[:, 0, 0], wide_out[:, 0, 1] = cosine, -sine
    wide_out[:, 1, 0], wide_out[:, 1, 1] = sine, cosine
    block_out = np.concatenate([np.cos(spread.T), -np.sin(spread.T)], 1)
    made = (
        block_in,
        wide_in.reshape(2 * WIDE, 2 * WIDE),
        tap_in.reshape(2, 2 * WIDE, 2 * BLOCKS),
        wide_out.reshape(2 * BLOCKS, 2 * WIDE) / WIDE,
        block_out / FREQ,
    )
    return [table.astype(np.float32).astype(ml_dtypes.bfloat16) for table in made]


def dot(left, right):
    return jnp.dot(left, right, preferred_element_type=F32)


def rows(start, count=LANE, align=8):
    return pl.ds(pl.multiple_of(start, align), count)


def kernel(
    in_gate, values, taps, skip, out_gate, *rest
):
    table_refs, rest = rest[:5], rest[5:]
    result, gate_a, gate_b, gate_c, mixed, skip_here, *rest = rest
    (block_in, wide_in, tap_in, wide_out, block_out), rest = rest[:5], rest[5:]
    (
        gated, own, before, all_taps, filtered, returned,
        signal_rows, tap_rows, tap_spectrum, product, answer_rows,
        load_sem, go_send, go_recv, pass_send, pass_recv, tap_send, tap_recv, twin_send, twin_recv,
        back_send, back_recv, out_sem,
    ) = rest
    s, v = lax.axis_index("seq"), lax.axis_index("wide")
    z, x = v // 4, v % 4
    twin = s + 1 - 2 * (s % 2)

    def near(i):
        return (8 + (2 * (i % 2) - 1) * ((i + 1) // 2)) % 8

    def ahead(k):
        return (z + k // 4) % 8 * 4 + (x + k % 4) % 4

    def behind(k):
        return (z + 8 - k // 4) % 8 * 4 + (x + 4 - k % 4) % 4

    here = (in_gate, values, taps, *table_refs, skip, out_gate)
    there = (gate_a, gate_b, all_taps.at[s], block_in, wide_in, tap_in, wide_out, block_out, skip_here, gate_c)
    loads = [
        pltpu.make_async_copy(source, target, load_sem.at[i])
        for i, (source, target) in enumerate(zip(here, there))
    ]
    for load in loads:
        load.start()

    barrier = pltpu.get_barrier_semaphore()

    def greet(k, carry):
        pl.semaphore_signal(barrier, inc=1, device_id={"wide": behind(k)}, device_id_type=MESH)
        return carry

    lax.fori_loop(1, BLOCKS, greet, 0)
    for other in ((s + GROUPS - 2) % GROUPS, (s + 2) % GROUPS, twin, (s + GROUPS - 1) % GROUPS):
        pl.semaphore_signal(barrier, inc=1, device_id={"seq": other}, device_id_type=MESH)

    def go(k):
        return pltpu.make_async_remote_copy(
            src_ref=gated.at[ahead(k)], dst_ref=own.at[v],
            send_sem=go_send.at[k], recv_sem=go_recv.at[k],
            device_id={"wide": ahead(k)}, device_id_type=MESH,
        )

    def pass_on(step):
        blocks = pl.ds((z + 8 - step) % 8 * 4, 4)
        return pltpu.make_async_remote_copy(
            src_ref=own.at[blocks], dst_ref=before.at[blocks],
            send_sem=pass_send.at[step], recv_sem=pass_recv.at[step],
            device_id={"seq": (s + 1) % GROUPS}, device_id_type=MESH,
        )

    def tap_group(i):
        return (s + (GROUPS - 2 * i if i <= 4 else 2 * (i - 4))) % GROUPS

    def tap_go(i):
        away = 2 if i <= 4 else GROUPS - 2
        held = all_taps.at[(tap_group(i) + away) % GROUPS]
        return pltpu.make_async_remote_copy(
            src_ref=held, dst_ref=held,
            send_sem=tap_send.at[i], recv_sem=tap_recv.at[i],
            device_id={"seq": (s + away) % GROUPS}, device_id_type=MESH,
        )

    def tap_twin(i):
        held = all_taps.at[tap_group(i)]
        return pltpu.make_async_remote_copy(
            src_ref=held, dst_ref=held,
            send_sem=twin_send.at[i], recv_sem=twin_recv.at[i],
            device_id={"seq": twin}, device_id_type=MESH,
        )

    def back(k):
        return pltpu.make_async_remote_copy(
            src_ref=filtered.at[ahead(k)], dst_ref=returned.at[v],
            send_sem=back_send.at[k], recv_sem=back_recv.at[k],
            device_id={"wide": ahead(k)}, device_id_type=MESH,
        )

    pl.semaphore_wait(barrier, BLOCKS - 1 + 4)
    loads[2].wait()
    tap_go(1).start()
    tap_go(5).start()
    tap_twin(0).start()
    loads[0].wait()
    loads[1].wait()

    def gate(u):
        columns = rows(u * LANE, align=LANE)
        gated[u] = (gate_a[:, columns].astype(F32) * gate_b[:, columns].astype(F32)).astype(BF16)

    def send_go(i, carry):
        step = near(i)
        for j in range(4):
            k = 4 * step + j
            gate(ahead(k))

            @pl.when(k > 0)
            def _():
                go(k).start()

        return carry

    lax.fori_loop(0, 8, send_go, 0)
    own[v] = gated[v]
    for load in loads[3:]:
        load.wait()

    def block_spectrum(source, target, at):
        spectrum = dot(block_in[...], source)
        target[rows(at * 2 * PITCH), :] = spectrum[:FREQ]
        target[rows(at * 2 * PITCH + PITCH), :] = spectrum[FREQ:]

    def pair(source, k, count):
        first = source[pl.ds(k, count, stride=PITCH), :]
        second = source[pl.ds(k + FREQ // 2, count, stride=PITCH), :]
        return jnp.concatenate([first, second], axis=1).astype(BF16)

    for i in (1, 5, 2, 6, 3, 7, 4):
        tap_go(i).wait_recv()
        if i not in (4, 7):
            tap_go(i + 1).start()
        tap_twin(i).start()
    for i in range(8):
        tap_twin(i).wait_recv()

    def tap_block(i, carry):
        for j in range(4):
            block = all_taps[2 * i + j // 2, j % 2 * LANE : (j % 2 + 1) * LANE]
            block_spectrum(block, tap_rows, 4 * i + j)
        return carry

    lax.fori_loop(0, 8, tap_block, 0)

    def tap_wide(i, carry):
        for p in range(16):
            k = 16 * i + p
            tap_spectrum[k] = dot(tap_in[p % 2], pair(tap_rows, k, 2 * BLOCKS))
        return carry

    lax.fori_loop(0, 4, tap_wide, 0)

    def arrive(i):
        step = near(i)
        for j in range(4):
            @pl.when(4 * step + j > 0)
            def _():
                go(4 * step + j).wait_recv()
        pass_on(step).start()
        for j in range(4):
            at = (z + 8 - step) % 8 * 4 + j
            block_spectrum(own[at], signal_rows, BLOCKS + at)

    def arrive_before(i):
        step = near(i)
        pass_on(step).wait_recv()
        for j in range(4):
            at = (z + 8 - step) % 8 * 4 + j
            block = before[at]
            block_spectrum(jnp.where(s > 0, block, jnp.zeros_like(block)), signal_rows, at)

    def first(i, carry):
        arrive(i)
        return carry

    def both(i, carry):
        arrive(i)
        arrive_before(i - LAG)
        return carry

    def last(i, carry):
        arrive_before(i)
        return carry

    lax.fori_loop(0, LAG, first, 0)
    lax.fori_loop(LAG, 8, both, 0)
    lax.fori_loop(8 - LAG, 8, last, 0)

    def multiply(i, carry):
        for p in range(32):
            k = 32 * i + p
            signal = dot(wide_in[...], pair(signal_rows, k, 2 * WIDE))
            tap = tap_spectrum[k]
            real, imag, tap_real, tap_imag = signal[:WIDE], signal[WIDE:], tap[:WIDE], tap[WIDE:]
            product[k] = jnp.concatenate(
                [real * tap_real - imag * tap_imag, real * tap_imag + imag * tap_real], axis=0
            ).astype(BF16)
        return carry

    lax.fori_loop(0, 2, multiply, 0)

    def wide_back(i, carry):
        for p in range(16):
            k = 16 * i + p
            answer = dot(wide_out[...], product[k])
            answer_rows[pl.ds(k, 2 * BLOCKS, stride=PITCH), :] = answer[:, :LANE]
            answer_rows[pl.ds(k + FREQ // 2, 2 * BLOCKS, stride=PITCH), :] = answer[:, LANE:]
        return carry

    lax.fori_loop(0, 4, wide_back, 0)

    def finish(i, carry):
        for p in range(4):
            at = ahead(4 * near(i) + p)
            spectrum = jnp.concatenate(
                [answer_rows[rows(at * 2 * PITCH), :], answer_rows[rows(at * 2 * PITCH + PITCH), :]], axis=0
            ).astype(BF16)
            direct = skip_here[...] * own[at].astype(F32)
            filtered[at] = (dot(block_out[...], spectrum) + direct).astype(BF16)
        for p in range(4):
            k = 4 * near(i) + p

            @pl.when(k > 0)
            def _():
                back(k).start()
        return carry

    lax.fori_loop(0, BLOCKS // 4, finish, 0)
    returned[v] = filtered[v]

    def output(at):
        columns = rows(at * LANE, align=LANE)
        mixed[:, columns] = (gate_c[:, columns].astype(F32) * returned[at].astype(F32)).astype(BF16)

    def drain(k, carry):
        go(k).wait_send()
        return carry

    lax.fori_loop(1, BLOCKS, drain, 0)
    for i in range(8):
        pass_on(i).wait_send()
        tap_twin(i).wait_send()
    for i in range(1, 8):
        tap_go(i).wait_send()

    def write(i):
        columns = rows((z + 8 - near(i)) % 8 * 4 * LANE, 4 * LANE, LANE)
        return pltpu.make_async_copy(mixed.at[:, columns], result.at[:, columns], out_sem.at[i])

    def arrive_back(i, carry):
        for j in range(4):
            k = 4 * near(i) + j

            @pl.when(k > 0)
            def _():
                back(k).wait_recv()

        for j in range(4):
            output(behind(4 * near(i) + j))
        write(i).start()
        for j in range(4):
            k = 4 * near(i) + j

            @pl.when(k > 0)
            def _():
                back(k).wait_send()

        return carry

    lax.fori_loop(0, 8, arrive_back, 0)

    for i in range(8):
        write(i).wait()


def local(out_gate, in_gate, values, filter_taps, skip_gain):
    anywhere = pl.BlockSpec(memory_space=pl.ANY)
    block = (BLOCKS, LANE, LANE)
    many, eight = pltpu.SemaphoreType.DMA((BLOCKS,)), pltpu.SemaphoreType.DMA((8,))
    made = tables()
    mixed = pl.pallas_call(
        kernel,
        out_shape=jax.ShapeDtypeStruct(out_gate.shape, BF16),
        in_specs=[anywhere] * (5 + len(made)),
        out_specs=anywhere,
        scratch_shapes=[pltpu.VMEM(out_gate.shape, BF16)] * 4
        + [pltpu.VMEM((1, LANE), F32)]
        + [pltpu.VMEM(table.shape, BF16) for table in made]
        + [pltpu.VMEM(block, BF16)] * 3
        + [pltpu.VMEM((GROUPS, 2 * LANE, LANE), BF16)]
        + [pltpu.VMEM(block, BF16)] * 2
        + [
            pltpu.VMEM((2 * WIDE * PITCH, LANE), F32),
            pltpu.VMEM((2 * BLOCKS * PITCH, LANE), F32),
            pltpu.VMEM((FREQ // 2, 2 * WIDE, 2 * LANE), F32),
            pltpu.VMEM((FREQ // 2, 2 * WIDE, 2 * LANE), BF16),
            pltpu.VMEM((2 * BLOCKS * PITCH, LANE), F32),
            pltpu.SemaphoreType.DMA((5 + len(made),)),
            many, many, eight, eight, eight, eight, eight, eight, many, many, eight,
        ],
        compiler_params=pltpu.CompilerParams(
            collective_id=0, has_side_effects=True, vmem_limit_bytes=58 << 20
        ),
    )(in_gate, values, filter_taps, skip_gain[None, :], out_gate, *made)
    return mixed


def solution(mesh):
    rows_split = P(("seq", "wide"), None)
    return jax.shard_map(
        local,
        mesh=mesh,
        in_specs=(rows_split, rows_split, rows_split, P("seq", "wide"), P("wide")),
        out_specs=rows_split,
        check_vma=False,
    )
```

```python
import jax
import jax.numpy as jnp
import ml_dtypes
import numpy as np
from jax import lax
from jax.experimental import pallas as pl
from jax.experimental.pallas import tpu as pltpu
from jax.sharding import PartitionSpec as P

MESH = pl.DeviceIdType.MESH
F32, BF16 = jnp.float32, jnp.bfloat16

LANE = 128
BLOCKS = 32
GROUPS = 16
FREQ = 128
WIDE = 64
LAG = 6
PITCH = FREQ + 8


def tables():
    k, b, m = np.arange(FREQ), np.arange(LANE), np.arange(WIDE)
    angle = np.pi * (2 * k + 1) / 256
    wide_angle = 2 * np.pi * (np.outer(m, m) % WIDE) / WIDE

    spread = np.outer(angle, b)
    block_in = np.concatenate([np.cos(spread), -np.sin(spread)], 0)
    cosine, sine = np.cos(wide_angle), np.sin(wide_angle)
    wide_in = np.zeros((2, WIDE, WIDE, 2))
    wide_in[0, :, :, 0], wide_in[0, :, :, 1] = cosine, sine
    wide_in[1, :, :, 0], wide_in[1, :, :, 1] = -sine, cosine

    turn = np.exp(-1j * wide_angle)[:, :BLOCKS]
    tap_in = np.zeros((2, 2, WIDE, BLOCKS, 2))
    for parity, sign in ((0, 1.0), (1, -1.0)):
        factor = (1 + 1j * sign * np.exp(-2j * np.pi * m / WIDE))[:, None] * turn
        tap_in[parity, 0, :, :, 0], tap_in[parity, 0, :, :, 1] = factor.real, -factor.imag
        tap_in[parity, 1, :, :, 0], tap_in[parity, 1, :, :, 1] = factor.imag, factor.real

    wide_out = np.zeros((BLOCKS, 2, 2, WIDE))
    cosine, sine = cosine[BLOCKS:], sine[BLOCKS:]
    wide_out[:, 0, 0], wide_out[:, 0, 1] = cosine, -sine
    wide_out[:, 1, 0], wide_out[:, 1, 1] = sine, cosine
    block_out = np.concatenate([np.cos(spread.T), -np.sin(spread.T)], 1)
    made = (
        block_in,
        wide_in.reshape(2 * WIDE, 2 * WIDE),
        tap_in.reshape(2, 2 * WIDE, 2 * BLOCKS),
        wide_out.reshape(2 * BLOCKS, 2 * WIDE) / WIDE,
        block_out / FREQ,
    )
    return [table.astype(np.float32).astype(ml_dtypes.bfloat16) for table in made]


def dot(left, right):
    return jnp.dot(left, right, preferred_element_type=F32)


def rows(start, count=LANE, align=8):
    return pl.ds(pl.multiple_of(start, align), count)


def kernel(
    in_gate, values, taps, skip, out_gate, *rest
):
    table_refs, rest = rest[:5], rest[5:]
    result, gate_a, gate_b, gate_c, mixed, skip_here, *rest = rest
    (block_in, wide_in, tap_in, wide_out, block_out), rest = rest[:5], rest[5:]
    (
        gated, own, before, all_taps, filtered, returned,
        signal_rows, tap_rows, tap_spectrum, product, answer_rows,
        load_sem, go_send, go_recv, pass_send, pass_recv, tap_send, tap_recv, twin_send, twin_recv,
        back_send, back_recv, out_sem,
    ) = rest
    s, v = lax.axis_index("seq"), lax.axis_index("wide")
    z, x = v // 4, v % 4
    twin = s + 1 - 2 * (s % 2)

    def near(i):
        return (8 + (2 * (i % 2) - 1) * ((i + 1) // 2)) % 8

    def ahead(k):
        return lax.rem(z + k // 4, 8) * 4 + lax.rem(x + k % 4, 4)

    def behind(k):
        return lax.rem(z + 8 - k // 4, 8) * 4 + lax.rem(x + 4 - k % 4, 4)

    here = (in_gate, values, taps, *table_refs, skip, out_gate)
    there = (gate_a, gate_b, all_taps.at[s], block_in, wide_in, tap_in, wide_out, block_out, skip_here, gate_c)
    loads = [
        pltpu.make_async_copy(source, target, load_sem.at[i])
        for i, (source, target) in enumerate(zip(here, there))
    ]
    for load in loads:
        load.start()

    barrier = pltpu.get_barrier_semaphore()

    for k in range(1, BLOCKS):
        pl.semaphore_signal(barrier, inc=1, device_id={"wide": behind(k)}, device_id_type=MESH)
    for other in ((s + GROUPS - 2) % GROUPS, (s + 2) % GROUPS, twin, (s + GROUPS - 1) % GROUPS):
        pl.semaphore_signal(barrier, inc=1, device_id={"seq": other}, device_id_type=MESH)

    def go(k):
        return pltpu.make_async_remote_copy(
            src_ref=gated.at[ahead(k)], dst_ref=own.at[v],
            send_sem=go_send.at[k], recv_sem=go_recv.at[k],
            device_id={"wide": ahead(k)}, device_id_type=MESH,
        )

    def pass_on(step):
        blocks = pl.ds((z + 8 - step) % 8 * 4, 4)
        return pltpu.make_async_remote_copy(
            src_ref=own.at[blocks], dst_ref=before.at[blocks],
            send_sem=pass_send.at[step], recv_sem=pass_recv.at[step],
            device_id={"seq": (s + 1) % GROUPS}, device_id_type=MESH,
        )

    def tap_group(i):
        return (s + (GROUPS - 2 * i if i <= 4 else 2 * (i - 4))) % GROUPS

    def tap_go(i):
        away = 2 if i <= 4 else GROUPS - 2
        held = all_taps.at[(tap_group(i) + away) % GROUPS]
        return pltpu.make_async_remote_copy(
            src_ref=held, dst_ref=held,
            send_sem=tap_send.at[i], recv_sem=tap_recv.at[i],
            device_id={"seq": (s + away) % GROUPS}, device_id_type=MESH,
        )

    def tap_twin(i):
        held = all_taps.at[tap_group(i)]
        return pltpu.make_async_remote_copy(
            src_ref=held, dst_ref=held,
            send_sem=twin_send.at[i], recv_sem=twin_recv.at[i],
            device_id={"seq": twin}, device_id_type=MESH,
        )

    def back(k):
        return pltpu.make_async_remote_copy(
            src_ref=filtered.at[ahead(k)], dst_ref=returned.at[v],
            send_sem=back_send.at[k], recv_sem=back_recv.at[k],
            device_id={"wide": ahead(k)}, device_id_type=MESH,
        )

    pl.semaphore_wait(barrier, BLOCKS - 1 + 4)
    loads[2].wait()
    tap_go(1).start()
    tap_go(5).start()
    tap_twin(0).start()
    loads[0].wait()
    loads[1].wait()

    def gate(u):
        columns = rows(u * LANE, align=LANE)
        gated[u] = (gate_a[:, columns].astype(F32) * gate_b[:, columns].astype(F32)).astype(BF16)

    for i in range(8):
        for k in range(4 * (0, 1, 7, 2, 6, 3, 5, 4)[i], 4 * (0, 1, 7, 2, 6, 3, 5, 4)[i] + 4):
            gate(ahead(k))
            if k > 0:
                go(k).start()
    own[v] = gated[v]
    for load in loads[3:]:
        load.wait()

    def block_spectrum(source, target, at):
        spectrum = dot(block_in[...], source)
        target[rows(at * 2 * PITCH), :] = spectrum[:FREQ]
        target[rows(at * 2 * PITCH + PITCH), :] = spectrum[FREQ:]

    def pair(source, k, count):
        first = source[pl.ds(k, count, stride=PITCH), :]
        second = source[pl.ds(k + FREQ // 2, count, stride=PITCH), :]
        return jnp.concatenate([first, second], axis=1).astype(BF16)

    for i in (1, 5, 2, 6, 3, 7, 4):
        tap_go(i).wait_recv()
        if i not in (4, 7):
            tap_go(i + 1).start()
        tap_twin(i).start()
    for i in range(8):
        tap_twin(i).wait_recv()

    def tap_block(i, carry):
        for j in range(4):
            block = all_taps[2 * i + j // 2, j % 2 * LANE : (j % 2 + 1) * LANE]
            block_spectrum(block, tap_rows, 4 * i + j)
        return carry

    lax.fori_loop(0, 8, tap_block, 0)

    def tap_wide(i, carry):
        for p in range(16):
            k = 16 * i + p
            tap_spectrum[k] = dot(tap_in[p % 2], pair(tap_rows, k, 2 * BLOCKS))
        return carry

    lax.fori_loop(0, 4, tap_wide, 0)

    def arrive(i):
        step = near(i)
        for j in range(4):
            @pl.when(4 * step + j > 0)
            def _():
                go(4 * step + j).wait_recv()
        pass_on(step).start()
        for j in range(4):
            at = (z + 8 - step) % 8 * 4 + j
            block_spectrum(own[at], signal_rows, BLOCKS + at)

    def arrive_before(i):
        step = near(i)
        pass_on(step).wait_recv()
        for j in range(4):
            at = (z + 8 - step) % 8 * 4 + j
            block = before[at]
            block_spectrum(jnp.where(s > 0, block, jnp.zeros_like(block)), signal_rows, at)

    def first(i, carry):
        arrive(i)
        return carry

    def both(i, carry):
        arrive(i)
        arrive_before(i - LAG)
        return carry

    def last(i, carry):
        arrive_before(i)
        return carry

    lax.fori_loop(0, LAG, first, 0)
    lax.fori_loop(LAG, 8, both, 0)
    lax.fori_loop(8 - LAG, 8, last, 0)

    def multiply(i, carry):
        for p in range(32):
            k = 32 * i + p
            signal = dot(wide_in[...], pair(signal_rows, k, 2 * WIDE))
            tap = tap_spectrum[k]
            real, imag, tap_real, tap_imag = signal[:WIDE], signal[WIDE:], tap[:WIDE], tap[WIDE:]
            product[k] = jnp.concatenate(
                [real * tap_real - imag * tap_imag, real * tap_imag + imag * tap_real], axis=0
            ).astype(BF16)
        return carry

    lax.fori_loop(0, 2, multiply, 0)

    def wide_back(i, carry):
        for p in range(16):
            k = 16 * i + p
            answer = dot(wide_out[...], product[k])
            answer_rows[pl.ds(k, 2 * BLOCKS, stride=PITCH), :] = answer[:, :LANE]
            answer_rows[pl.ds(k + FREQ // 2, 2 * BLOCKS, stride=PITCH), :] = answer[:, LANE:]
        return carry

    lax.fori_loop(0, 4, wide_back, 0)

    def finish(i, carry):
        for p in range(4):
            at = ahead(4 * near(i) + p)
            spectrum = jnp.concatenate(
                [answer_rows[rows(at * 2 * PITCH), :], answer_rows[rows(at * 2 * PITCH + PITCH), :]], axis=0
            ).astype(BF16)
            direct = skip_here[...] * own[at].astype(F32)
            filtered[at] = (dot(block_out[...], spectrum) + direct).astype(BF16)
        for p in range(4):
            k = 4 * near(i) + p

            @pl.when(k > 0)
            def _():
                back(k).start()
        return carry

    lax.fori_loop(0, BLOCKS // 4, finish, 0)
    returned[v] = filtered[v]

    def output(at):
        columns = rows(at * LANE, align=LANE)
        mixed[:, columns] = (gate_c[:, columns].astype(F32) * returned[at].astype(F32)).astype(BF16)

    def drain(k, carry):
        go(k).wait_send()
        return carry

    lax.fori_loop(1, BLOCKS, drain, 0)
    for i in range(8):
        pass_on(i).wait_send()
        tap_twin(i).wait_send()
    for i in range(1, 8):
        tap_go(i).wait_send()

    def write(i):
        columns = rows((z + 8 - near(i)) % 8 * 4 * LANE, 4 * LANE, LANE)
        return pltpu.make_async_copy(mixed.at[:, columns], result.at[:, columns], out_sem.at[i])

    def arrive_back(i, carry):
        for j in range(4):
            k = 4 * near(i) + j

            @pl.when(k > 0)
            def _():
                back(k).wait_recv()

        for j in range(4):
            output(behind(4 * near(i) + j))
        write(i).start()
        for j in range(4):
            k = 4 * near(i) + j

            @pl.when(k > 0)
            def _():
                back(k).wait_send()

        return carry

    lax.fori_loop(0, 8, arrive_back, 0)

    for i in range(8):
        write(i).wait()


def local(out_gate, in_gate, values, filter_taps, skip_gain):
    anywhere = pl.BlockSpec(memory_space=pl.ANY)
    block = (BLOCKS, LANE, LANE)
    many, eight = pltpu.SemaphoreType.DMA((BLOCKS,)), pltpu.SemaphoreType.DMA((8,))
    made = tables()
    mixed = pl.pallas_call(
        kernel,
        out_shape=jax.ShapeDtypeStruct(out_gate.shape, BF16),
        in_specs=[anywhere] * (5 + len(made)),
        out_specs=anywhere,
        scratch_shapes=[pltpu.VMEM(out_gate.shape, BF16)] * 4
        + [pltpu.VMEM((1, LANE), F32)]
        + [pltpu.VMEM(table.shape, BF16) for table in made]
        + [pltpu.VMEM(block, BF16)] * 3
        + [pltpu.VMEM((GROUPS, 2 * LANE, LANE), BF16)]
        + [pltpu.VMEM(block, BF16)] * 2
        + [
            pltpu.VMEM((2 * WIDE * PITCH, LANE), F32),
            pltpu.VMEM((2 * BLOCKS * PITCH, LANE), F32),
            pltpu.VMEM((FREQ // 2, 2 * WIDE, 2 * LANE), F32),
            pltpu.VMEM((FREQ // 2, 2 * WIDE, 2 * LANE), BF16),
            pltpu.VMEM((2 * BLOCKS * PITCH, LANE), F32),
            pltpu.SemaphoreType.DMA((5 + len(made),)),
            many, many, eight, eight, eight, eight, eight, eight, many, many, eight,
        ],
        compiler_params=pltpu.CompilerParams(
            collective_id=0, has_side_effects=True, vmem_limit_bytes=58 << 20
        ),
    )(in_gate, values, filter_taps, skip_gain[None, :], out_gate, *made)
    return mixed


def solution(mesh):
    rows_split = P(("seq", "wide"), None)
    return jax.shard_map(
        local,
        mesh=mesh,
        in_specs=(rows_split, rows_split, rows_split, P("seq", "wide"), P("wide")),
        out_specs=rows_split,
        check_vma=False,
    )
```
